512 devices in a mesh: expert: 16 (over x_hi, y, core), tensor: 32 (over x_lo, z).
Axes of the slice: x: 4 (x_hi: 2, x_lo: 2; x = x_hi * 2 + x_lo), y: 4, z: 16, core: 2. Of those that a mesh axis runs over, the one named last changes fastest.
Arguments:
- token_grads: bfloat16 [2048, 5120], P('expert', 'tensor'), may hold values from -4 to 4
- combine: float32 [2048, 6], P('expert'), may hold values from 0.1 to 1
- routes: int32 [2048, 6], P('expert'), may hold values from 0 to 15, all different within a row; in each aligned block of 128 rows (0 to 127, 128 to 255, ...) at most 96 rows name the same one
- bin_inputs: bfloat16 [16, 1024, 5120], P('expert', None, 'tensor'), may hold values from -6 to 6
- gate_pre: bfloat16 [16, 1536, 1024], P('expert', 'tensor'), may hold values from -6 to 6
- up_pre: bfloat16 [16, 1536, 1024], P('expert', 'tensor'), may hold values from -6 to 6
- gate_weight: bfloat16 [16, 5120, 1536], P('expert', 'tensor'), may hold values from -0.15625 to 0.15625
- up_weight: bfloat16 [16, 5120, 1536], P('expert', 'tensor'), may hold values from -0.15625 to 0.15625
- down_weight: bfloat16 [16, 5120, 1536], P('expert', 'tensor'), may hold values from -0.078125 to 0.078125
Outputs:
- token_grad: bfloat16 [2048, 5120], P('expert', 'tensor')
- gate_grad: bfloat16 [16, 5120, 1536], P('expert', 'tensor')
- up_grad: bfloat16 [16, 5120, 1536], P('expert', 'tensor')
- down_grad: bfloat16 [16, 5120, 1536], P('expert', 'tensor')
The draws below stay inside these ranges and needn't reach their ends.
Inputs may be any that keep to these rules, and one draw needn't show every extreme that they name: `routes`: each token names 6 different experts. Within the 128 tokens of one index of the expert axis no expert is named by more than 96 tokens.
All inputs are finite; a program needn't handle non-finite values.
Results may differ from the reference program's by a relative error of at most 0.0064.
Values may be sent and summed in bfloat16 or wider, within the bound.
A program may use at most 64 MiB of HBM per device.

```python
import math
import jax
import jax.numpy as jnp
import numpy as np
from jax import lax

D = 5120
FF = 1536
TOP = 6
EXPERTS = 16
TOK_G = 128
CAP = 64
ROUTE_MOST = 96
BINS = 1024
TOKENS = 2048
N_EXPERT = 16


def shard_levels(key, extent, shards, least, high):
    loudness = 1.0
    for dim, parts in shards:
        heights = jax.random.uniform(jax.random.fold_in(jax.random.fold_in(key, 6), dim), (parts,), jnp.float32, least / len(shards), high / len(shards))
        loudness = loudness * jnp.repeat(jnp.exp(heights), extent[dim] // parts).reshape((-1,) + (1,) * (len(extent) - 1 - dim))
    return loudness


def shared_out(stream_key, own, number, rows, number_of, top, limit, lean):
    order = jax.random.permutation(stream_key, number_of)
    heavy_load, usual = portions_of(number_of, rows * top, limit, lean, True), portions_of(number_of, rows * top, limit, lean, False)
    places = jnp.arange(number_of)

    def named(lengths, offset_by):
        used = int((lengths > 0).sum())
        fixed = max(1, used // 4)
        passed = fixed + (places - fixed + offset_by * (used - fixed)) % max(1, number_of - fixed)
        return jnp.zeros((number_of,), jnp.int32).at[order[jnp.where(places < fixed, places, passed)]].set(jnp.asarray(lengths, jnp.int32))

    lengths = jnp.where(number % 4 == 0, named(heavy_load, number // 4), named(usual, number - number // 4 - 1))
    mixed = jax.random.permutation(jax.random.fold_in(own, 3), number_of)
    source_of, receiver = mixed[0:number_of // 2 * 2:2], mixed[1:number_of // 2 * 2:2]
    slack = jnp.minimum(lengths[source_of] - 1, limit - lengths[receiver]) // 2
    slack = jnp.where((source_of == order[0]) | (receiver == order[0]) | (lengths[receiver] == 0), 0, jnp.maximum(slack, 0))
    passed = jax.random.randint(jax.random.fold_in(own, 4), (number_of // 2,), 0, 1 << 20) % (slack + 1)
    lengths = lengths.at[source_of].add(-passed).at[receiver].add(passed)
    members = jnp.searchsorted(jnp.cumsum(lengths), jnp.arange(rows * top), side="right").astype(jnp.int32)
    listing = members.reshape(top, rows).T
    listing = listing[jax.random.permutation(jax.random.fold_in(own, 1), rows)]
    offset_by = jax.random.randint(jax.random.fold_in(own, 2), (rows, 1), 0, top)
    return jnp.take_along_axis(listing, (jnp.arange(top)[None, :] + offset_by) % top, axis=1)


def portions_of(number_of, total, reach, lean, full):
    portions = [(1 << 20) // math.isqrt(rank ** lean) + 1 for rank in range(1, number_of + 1)]
    largest = reach if full else min(reach, max(-(-total // number_of), total * portions[0] // sum(portions)))
    least = 1 if total - largest >= number_of - 1 else 0
    holding, surplus = [largest] + [least] * (number_of - 1), total - largest - least * (number_of - 1)
    while surplus > 0:
        movable = [i for i in range(1, number_of) if holding[i] < largest] or [i for i in range(1, number_of) if holding[i] < reach]
        mass, budget = sum([portions[i] for i in movable]), surplus
        for i in movable:
            addition = min(reach - holding[i], max(1, budget * portions[i] // mass), surplus)
            holding[i] = holding[i] + addition
            surplus = surplus - addition
    return np.array(holding)


def gaussian(stream_key, extent, scale, bound, split=(), kind=jnp.bfloat16):
    entries = jax.random.normal(stream_key, extent, jnp.float32) * scale
    if len(split) > 0:
        entries = shard_levels(stream_key, extent, split, -0.22, 0.18) * entries
    return jnp.clip(entries, min=-bound, max=bound).astype(kind)


def setup_inputs(seed: int = 0) -> dict:
    key_of = jax.random.split(jax.random.key(seed), 10)
    token_grads = gaussian(key_of[0], (TOKENS, D), 0.5, 4.0, ((0, 16), (1, 32)))
    combine = jnp.clip(0.1 + 0.9 * jax.random.uniform(key_of[1], (TOKENS, TOP), jnp.float32) ** shard_levels(key_of[1], (TOKENS, TOP), ((0, 16),), -0.2, 0.2), 0.1, 1.0)
    routes_keys = jax.random.split(jax.random.fold_in(key_of[2], 1), TOKENS // TOK_G)
    routes_turns = jax.random.permutation(jax.random.fold_in(key_of[2], 3), TOKENS // TOK_G)
    routes = jax.vmap(lambda own, number: shared_out(jax.random.fold_in(key_of[2], 2), own, number, TOK_G, EXPERTS, TOP, ROUTE_MOST, 2))(routes_keys, routes_turns).reshape((TOKENS, TOP))
    bin_inputs = gaussian(key_of[3], (EXPERTS, BINS, D), 1.0, 6.0, ((0, 16), (2, 32)))
    gate_pre = gaussian(key_of[4], (EXPERTS, FF, BINS), 1.5, 6.0, ((0, 16), (1, 32)))
    up_pre = gaussian(key_of[5], (EXPERTS, FF, BINS), 1.0, 6.0, ((0, 16), (1, 32)))
    gate_weight = gaussian(key_of[6], (EXPERTS, D, FF), FF ** -0.5, 0.15625, ((0, 16), (1, 32)))
    up_weight = gaussian(key_of[7], (EXPERTS, D, FF), FF ** -0.5, 0.15625, ((0, 16), (1, 32)))
    down_weight = gaussian(key_of[8], (EXPERTS, D, FF), D ** -0.5, 0.078125, ((0, 16), (1, 32)))
    return dict(token_grads=token_grads, combine=combine, routes=routes, bin_inputs=bin_inputs, gate_pre=gate_pre, up_pre=up_pre, gate_weight=gate_weight, up_weight=up_weight, down_weight=down_weight)


def route_slots(block):
    flat_routes = block.reshape(-1).astype(jnp.int32)
    expert_ids = jnp.arange(EXPERTS, dtype=jnp.int32)
    onehot = (flat_routes[:, None] == expert_ids[None, :]).astype(jnp.int32)
    earlier = jnp.cumsum(onehot, axis=0) - onehot
    slot_rank = jnp.sum(earlier * onehot, axis=1).astype(jnp.int32)
    return flat_routes, slot_rank, slot_rank < CAP


def activate(hidden_grad, gate_pre, up_pre):
    gate_vals = gate_pre.astype(jnp.float32)
    up_vals = up_pre.astype(jnp.float32)
    sigmoid_gate = 1.0 / (1.0 + jnp.exp(-gate_vals))
    activated = gate_vals * sigmoid_gate
    hidden = (activated * up_vals).astype(jnp.bfloat16)
    up_delta = (hidden_grad * activated).astype(jnp.bfloat16)
    gate_delta = (hidden_grad * up_vals * sigmoid_gate * (1.0 + gate_vals * (1.0 - sigmoid_gate))).astype(jnp.bfloat16)
    return hidden, gate_delta, up_delta


def product(left, right):
    return jnp.dot(left.astype(jnp.float32), right.astype(jnp.float32), precision=lax.Precision.HIGHEST)


def reference(token_grads, combine, routes, bin_inputs, gate_pre, up_pre, gate_weight, up_weight, down_weight):
    bin_count = N_EXPERT * CAP
    blocks = routes.reshape(N_EXPERT, TOK_G * TOP)
    flat_routes, slot_rank, kept_mask = jax.vmap(route_slots)(blocks)
    source_ids = jnp.arange(N_EXPERT, dtype=jnp.int32)[:, None]
    bin_index = flat_routes * bin_count + source_ids * CAP + slot_rank
    bin_index = jnp.where(kept_mask, bin_index, EXPERTS * bin_count).astype(jnp.int32).reshape(-1)
    grad_rows = (combine[:, :, None] * token_grads.astype(jnp.float32)[:, None, :]).astype(jnp.bfloat16).reshape(-1, D)
    binned = jnp.zeros((EXPERTS * bin_count, D), jnp.bfloat16).at[bin_index].set(grad_rows, mode="drop")
    binned = binned.reshape(EXPERTS, bin_count, D)

    def expert_step(operands):
        grads_bin, inputs_bin, gate_part, up_part, gate_mat, up_mat, down_mat = operands
        hidden_grad = product(grads_bin, down_mat).T
        hidden, gate_delta, up_delta = activate(hidden_grad, gate_part, up_part)
        bin_back = (product(gate_delta.T, gate_mat.T) + product(up_delta.T, up_mat.T)).astype(jnp.bfloat16)
        down_part = product(grads_bin.T, hidden.T).astype(jnp.bfloat16)
        gate_part_grad = product(inputs_bin.T, gate_delta.T).astype(jnp.bfloat16)
        up_part_grad = product(inputs_bin.T, up_delta.T).astype(jnp.bfloat16)
        return bin_back, gate_part_grad, up_part_grad, down_part

    bin_back, gate_grad, up_grad, down_grad = lax.map(
        expert_step, (binned, bin_inputs, gate_pre, up_pre, gate_weight, up_weight, down_weight))
    flat_back = bin_back.reshape(EXPERTS * bin_count, D)
    picked = flat_back[jnp.minimum(bin_index, EXPERTS * bin_count - 1)].astype(jnp.float32)
    picked = jnp.where(kept_mask.reshape(-1)[:, None], picked, jnp.float32(0.0))
    token_grad = jnp.sum(picked.reshape(-1, TOP, D), axis=1).astype(jnp.bfloat16)
    return (token_grad, gate_grad, up_grad, down_grad)
```

```python
import functools

import jax
import jax.numpy as jnp
from jax import lax
from jax.experimental import pallas as pl
from jax.experimental.pallas import tpu as pltpu
from jax.sharding import PartitionSpec as P

CAP = 64
F32, BF16 = jnp.float32, jnp.bfloat16
MESH = pl.DeviceIdType.MESH
NT = (((1,), (1,)), ((), ()))

GATE, UP, SUM, ALL = range(4)
X_DOWN, X_GATE, X_UP, X_IN, X_DOWN_GRAD, X_GATE_GRAD, X_UP_GRAD = range(7)


def kernel(
    ne, nz,
    tg, combine, routes, bin_in, gate_pre, up_pre, gate_w, up_w, down_w,
    tok_out, gate_out, up_out, down_out,
    rc_r, rc_c, place, pick, placed, binned, down_x, gate_x, up_x, in_x,
    down_t, in_t, bin_t, part, sum_u, sum_d, first_u, first_d,
    gate_all, up_all, total_all, act_up, act_gate, hidden, gate_delta, up_delta,
    back, back_in, down_s, gate_s, up_s,
    su, ru, sd, rd, out_s, out_r, back_ss, back_r, xs, xr,
):
    e, t = lax.axis_index("expert"), lax.axis_index("tensor")
    xl, z = t // nz, lax.rem(t, nz)
    tokens, width = tg.shape
    top = routes.shape[1]
    fc, bins = gate_pre.shape
    half = fc * nz
    mine = pl.ds(pl.multiple_of(xl * half, 128), half)
    theirs = pl.ds(pl.multiple_of((1 - xl) * half, 128), half)

    def chunk(k):
        return lax.rem(z + k + 2 * nz, nz)

    above = (e, xl * nz + chunk(1))
    below = (e, xl * nz + chunk(-1))
    across = (e, (1 - xl) * nz + z)

    def partner(i):
        rel, de = lax.rem(i, 2), i // 2
        pe = lax.rem(e + de, ne)
        return rel, pe, (pe, lax.rem(xl + rel, 2) * nz + z)

    barrier = pltpu.get_barrier_semaphore()

    def greet(i, _):
        _, _, device = partner(i)
        pl.semaphore_signal(barrier, inc=1, device_id=device, device_id_type=MESH)
        return 0

    lax.fori_loop(1, 2 * ne, greet, 0)
    for device in (above, below):
        pl.semaphore_signal(barrier, inc=1, device_id=device, device_id_type=MESH)
    pl.semaphore_wait(barrier, 2 * ne + 1)

    def hop(ring, s, upward, src, dst):
        return pltpu.make_async_remote_copy(
            src_ref=src, dst_ref=dst,
            send_sem=(su if upward else sd).at[ring, s],
            recv_sem=(ru if upward else rd).at[ring, s],
            device_id=above if upward else below, device_id_type=MESH,
        )

    def gather_send(ring, buf, own, s, upward):
        k = chunk(-s if upward else s)
        hop(ring, s, upward, own if s == 0 else buf.at[k], buf.at[k]).start()

    def gather_recv(ring, buf, s, upward):
        k = chunk(-1 - s if upward else 1 + s)
        hop(ring, s, upward, buf.at[k], buf.at[k]).wait_recv()
        return k

    def exchange(i, src, dst):
        return pltpu.make_async_remote_copy(
            src_ref=src, dst_ref=dst, send_sem=xs.at[i], recv_sem=xr.at[i],
            device_id=across, device_id_type=MESH,
        )

    pre_u, pre_d = nz - 1 - nz // 2, nz // 2
    progress = [0]

    def pump():
        i = progress[0]
        s, ring = i // 2, i % 2
        if s > pre_d:
            return
        progress[0] += 1
        buf, own = ((gate_all, gate_pre), (up_all, up_pre))[ring]
        for upward, n in ((True, pre_u), (False, pre_d)):
            if 0 < s <= n:
                gather_recv(ring, buf, s - 1, upward)
            if s < n:
                gather_send(ring, buf, own, s, upward)
        if ring == 1 and s > 0:
            if s <= pre_u:
                activate(chunk(-s))
            activate(chunk(s))

    def activate(c):
        def rows(r, _):
            at = pl.ds(pl.multiple_of(r * 16, 16), 16)
            g, u = gate_all[c, at, :].astype(F32), up_all[c, at, :].astype(F32)
            s = 1.0 / (1.0 + jnp.exp(-g))
            a = g * s
            act_up[c, at, :] = a
            act_gate[c, at, :] = u * s * (1.0 + g * (1.0 - s))
            hidden[c, at, :] = (a * u).astype(BF16)
            return 0

        lax.fori_loop(0, fc // 16, rows, 0)

    def deltas(c):
        def rows(r, _):
            at = pl.ds(pl.multiple_of(r * 16, 16), 16)
            v = total_all[c, at, :].astype(F32)
            up_delta[c, at, :] = (v * act_up[c, at, :]).astype(BF16)
            gate_delta[c, at, :] = (v * act_gate[c, at, :]).astype(BF16)
            return 0

        lax.fori_loop(0, fc // 16, rows, 0)

    pump()
    pump()
    x_down = exchange(X_DOWN, down_w.at[:, theirs], down_x)
    x_down.start()

    rc_r[...] = jnp.zeros_like(rc_r)
    rc_c[...] = jnp.zeros_like(rc_c)
    rc_r[:, 0:top] = routes[...].astype(F32)
    rc_c[:, 0:top] = combine[...]
    r_t, c_t = rc_r[...].T, rc_c[...].T
    expert_ids = lax.broadcasted_iota(jnp.int32, (ne, tokens), 0).astype(F32)
    named = jnp.zeros((ne, tokens), F32)
    weight = jnp.zeros((ne, tokens), F32)
    for k in range(top):
        hit = r_t[k : k + 1, :] == expert_ids
        named = named + jnp.where(hit, 1.0, 0.0)
        weight = weight + jnp.where(hit, c_t[k : k + 1, :], 0.0)
    before = lax.broadcasted_iota(jnp.int32, (tokens, tokens), 0) < lax.broadcasted_iota(
        jnp.int32, (tokens, tokens), 1
    )
    earlier = jnp.dot(
        named.astype(BF16), jnp.where(before, 1.0, 0.0).astype(BF16), preferred_element_type=F32
    )
    slot = jnp.where(named > 0.5, earlier, -1.0)
    slot_ids = lax.broadcasted_iota(jnp.int32, (CAP, tokens), 0).astype(F32)
    for x in range(ne):
        hit = slot_ids == slot[x : x + 1, :]
        place[x] = jnp.where(hit, 1.0, 0.0)
        w = jnp.where(hit, weight[x : x + 1, :], 0.0)
        hi = w.astype(BF16)
        w = w - hi.astype(F32)
        mid = w.astype(BF16)
        lo = (w - mid.astype(F32)).astype(BF16)
        rows = (
            jnp.dot(hi, tg[...], preferred_element_type=F32)
            + jnp.dot(mid, tg[...], preferred_element_type=F32)
            + jnp.dot(lo, tg[...], preferred_element_type=F32)
        )
        placed[x] = rows.astype(BF16)

    def dispatch(i, _):
        rel, pe, device = partner(i)
        pltpu.make_async_remote_copy(
            src_ref=placed.at[pe], dst_ref=binned.at[rel * ne + e],
            send_sem=out_s, recv_sem=out_r, device_id=device, device_id_type=MESH,
        ).start()
        return 0

    lax.fori_loop(1, 2 * ne, dispatch, 0)
    binned[e] = placed[e]

    pump()
    pump()
    gate_all[z] = gate_pre[...]
    up_all[z] = up_pre[...]
    activate(z)
    down_t[0] = down_w[:, mine].T
    in_t[0] = bin_in[...].T
    pick[...] = place[...].reshape(ne * CAP, tokens).T.astype(BF16)
    pump()
    pump()
    x_down.wait_recv()
    down_t[1] = down_x[...].T

    many = binned.at[pl.ds(0, 2 * ne - 1)]
    pltpu.make_async_copy(many, many, out_r).wait()
    x_gate = exchange(X_GATE, gate_w.at[:, theirs], gate_x)
    x_up = exchange(X_UP, up_w.at[:, theirs], up_x)
    x_in = exchange(X_IN, bin_in, in_x)
    for copy in (x_in, x_gate, x_up):
        copy.start()
    bin_0 = binned[0:ne].reshape(bins, width)
    bin_1 = binned[ne : 2 * ne].reshape(bins, width)
    part[...] = (
        lax.dot_general(down_t[0], bin_0, NT, preferred_element_type=F32)
        + lax.dot_general(down_t[1], bin_1, NT, preferred_element_type=F32)
    ).reshape(nz, fc, bins)

    nu, nd = nz // 2, nz - 1 - nz // 2
    first_u[...] = part[chunk(nu)].astype(BF16)
    hop(SUM, 0, True, first_u, sum_u.at[0]).start()
    first_d[...] = part[chunk(-nd)].astype(BF16)
    hop(SUM, 0, False, first_d, sum_d.at[0]).start()
    bin_t[0] = bin_0.T
    bin_t[1] = bin_1.T
    for s in range(1, nu + 1):
        for upward, n, buf in ((True, nu, sum_u), (False, nd, sum_d)):
            if s <= n:
                hop(SUM, s - 1, upward, buf.at[s - 1], buf.at[s - 1]).wait_recv()
            if s < n:
                c = chunk(nu - s if upward else s - nd)
                buf[s - 1] = (buf[s - 1].astype(F32) + part[c]).astype(BF16)
                hop(SUM, s, upward, buf.at[s - 1], buf.at[s]).start()
        if s < nu:
            pump()
    total_all[z] = (
        part[z] + (sum_u[nu - 1].astype(F32) + sum_d[nd - 1].astype(F32))
    ).astype(BF16)

    for s in range(nu + 1):
        arrived = [z] if s == 0 else []
        for upward, n in ((True, nu), (False, nd)):
            if 0 < s <= n:
                arrived.append(gather_recv(ALL, total_all, s - 1, upward))
            if s < n:
                gather_send(ALL, total_all, total_all.at[z], s, upward)
        while progress[0] < 2 * s + 2 and progress[0] < 2 * pre_d + 2:
            pump()
        pump()
        if s == 2:
            x_in.wait_recv()
            in_t[1] = in_x[...].T
        for c in arrived:
            deltas(c)

    gd = gate_delta[...].reshape(half, bins)
    ud = up_delta[...].reshape(half, bins)
    x_gate.wait_recv()
    x_up.wait_recv()
    for rel in (1, 0):
        gw = gate_x[...] if rel else gate_w[:, mine]
        uw = up_x[...] if rel else up_w[:, mine]
        b_t = jnp.dot(gw, gd, preferred_element_type=F32) + jnp.dot(uw, ud, preferred_element_type=F32)
        back[rel * ne : (rel + 1) * ne] = b_t.T.astype(BF16).reshape(ne, CAP, width)

    def give(i, _):
        rel, pe, device = partner(i)
        pltpu.make_async_remote_copy(
            src_ref=back.at[rel * ne + pe], dst_ref=back_in.at[rel * ne + e],
            send_sem=back_ss, recv_sem=back_r, device_id=device, device_id_type=MESH,
        ).start()
        return 0

    lax.fori_loop(1, 2 * ne, give, 0)
    back_in[e] = back[e]

    copies = []
    for i, left, right, stage, out in (
        (X_GATE_GRAD, in_t, gd, gate_s, gate_out),
        (X_UP_GRAD, in_t, ud, up_s, up_out),
        (X_DOWN_GRAD, bin_t, hidden[...].reshape(half, bins), down_s, down_out),
    ):
        stage[...] = lax.dot_general(left[1], right, NT, preferred_element_type=F32).astype(BF16)
        copy = exchange(i, stage, out.at[:, mine])
        copy.start()
        copies.append(copy)
        out[:, mine] = lax.dot_general(left[0], right, NT, preferred_element_type=F32).astype(BF16)

    many = back_in.at[pl.ds(0, 2 * ne - 1)]
    pltpu.make_async_copy(many, many, back_r).wait()
    token = jnp.dot(
        pick[...], back_in[0:ne].reshape(ne * CAP, width), preferred_element_type=F32
    ) + jnp.dot(pick[...], back_in[ne : 2 * ne].reshape(ne * CAP, width), preferred_element_type=F32)
    tok_out[...] = token.astype(BF16)

    for copy in copies:
        copy.wait_recv()
    many = placed.at[0:1]
    sent = binned.at[pl.ds(0, 2 * ne - 1)]
    pltpu.make_async_copy(sent, sent, out_s).wait()
    sent = back.at[pl.ds(0, 2 * ne - 1)]
    pltpu.make_async_copy(sent, sent, back_ss).wait()
    for copy in [x_down, x_gate, x_up, x_in] + copies:
        copy.wait_send()
    for ring, n_up, n_down in ((GATE, pre_u, pre_d), (UP, pre_u, pre_d), (SUM, nu, nd), (ALL, nu, nd)):
        for s in range(n_up):
            hop(ring, s, True, first_u, first_u).wait_send()
        for s in range(n_down):
            hop(ring, s, False, first_d, first_d).wait_send()


def layer(ne, nz, *args):
    tg, combine, routes, bin_in, gate_pre, up_pre, gate_w, up_w, down_w = args
    bin_in, gate_pre, up_pre, gate_w, up_w, down_w = (
        a.reshape(a.shape[1:]) for a in (bin_in, gate_pre, up_pre, gate_w, up_w, down_w)
    )
    tokens, width = tg.shape
    fc, bins = gate_pre.shape
    half, ff = fc * nz, gate_w.shape[1]
    nu, nd = nz // 2, nz - 1 - nz // 2
    V = pltpu.VMEM
    dma = pltpu.SemaphoreType.DMA
    scratch = [
        V((tokens, 128), F32), V((tokens, 128), F32),
        V((ne, CAP, tokens), F32), V((tokens, ne * CAP), BF16),
        V((ne, CAP, width), BF16), V((2 * ne, CAP, width), BF16),
        V((width, half), BF16), V((width, half), BF16), V((width, half), BF16), V((bins, width), BF16),
        V((2, half, width), BF16), V((2, width, bins), BF16), V((2, width, bins), BF16),
        V((nz, fc, bins), F32),
        V((nu, fc, bins), BF16), V((max(nd, 1), fc, bins), BF16), V((fc, bins), BF16), V((fc, bins), BF16),
        V((nz, fc, bins), BF16), V((nz, fc, bins), BF16), V((nz, fc, bins), BF16),
        V((nz, fc, bins), F32), V((nz, fc, bins), F32), V((nz, fc, bins), BF16),
        V((nz, fc, bins), BF16), V((nz, fc, bins), BF16),
        V((2 * ne, CAP, width), BF16), V((2 * ne, CAP, width), BF16),
        V((width, half), BF16), V((width, half), BF16), V((width, half), BF16),
        dma((4, nu)), dma((4, nu)), dma((4, nu)), dma((4, nu)),
        dma, dma, dma, dma, dma((7,)), dma((7,)),
    ]
    grad = jax.ShapeDtypeStruct((width, ff), BF16)
    vmem = pl.BlockSpec(memory_space=pltpu.VMEM)
    token, gate, up, down = pl.pallas_call(
        functools.partial(kernel, ne, nz),
        out_shape=(jax.ShapeDtypeStruct((tokens, width), BF16), grad, grad, grad),
        in_specs=[vmem] * 9,
        out_specs=(vmem,) * 4,
        scratch_shapes=scratch,
        compiler_params=pltpu.CompilerParams(
            collective_id=0, has_side_effects=True, vmem_limit_bytes=58 * 2**20
        ),
        cost_estimate=pl.CostEstimate(
            flops=12 * width * ff * bins, bytes_accessed=6 * 2**20, transcendentals=half * bins
        ),
    )(tg, combine, routes, bin_in, gate_pre, up_pre, gate_w, up_w, down_w)
    return token, gate[None], up[None], down[None]


def solution(mesh):
    ne, nz = mesh.shape["expert"], mesh.shape["tensor"] // 2
    return jax.shard_map(
        functools.partial(layer, ne, nz),
        mesh=mesh,
        in_specs=(
            P("expert", "tensor"),
            P("expert", None),
            P("expert", None),
            P("expert", None, "tensor"),
            P("expert", "tensor", None),
            P("expert", "tensor", None),
            P("expert", "tensor", None),
            P("expert", "tensor", None),
            P("expert", "tensor", None),
        ),
        out_specs=(
            P("expert", "tensor"),
            P("expert", "tensor", None),
            P("expert", "tensor", None),
            P("expert", "tensor", None),
        ),
        check_vma=False,
    )
```

```python
import functools

import jax
import jax.numpy as jnp
from jax import lax
from jax.experimental import pallas as pl
from jax.experimental.pallas import tpu as pltpu
from jax.sharding import PartitionSpec as P

CAP = 64
LANES = 128
F32, BF16 = jnp.float32, jnp.bfloat16
MESH = pl.DeviceIdType.MESH
NT = (((1,), (1,)), ((), ()))

GATE, UP, SUM, ALL = 0, 1, (2, 3), (4, 5)
EARLY, BESIDE = 6, 1
LAG = 0


def nt(left, right):
    return lax.dot_general(left, right, NT, preferred_element_type=F32)


def nn(left, right):
    return jnp.dot(left, right, preferred_element_type=F32)


def kernel(
    ne, nz,
    tg, combine, routes, bin_in_h, gate_pre, up_pre, gate_w, up_w, down_w,
    tok_out, gate_out, up_out, down_out,
    bin_in, gate_m, up_m, down_m,
    place, pick, split, tail_t, placed, binned, bin_r, back, back_in, tok_r,
    down_x, gate_x, up_x, in_x, down_t, down_tr, bin_t, part,
    sum_u, sum_d, first_u, first_d, gate_all, up_all, total_all,
    act_up, act_gate, hidden, gate_delta, up_delta,
    down_s, strip, strip_in, grad_t, grad_tr,
    su, ru, sd, rd, out_s, out_r, back_s, back_r, xs, xr, ss, sr, ls,
):
    e, t = lax.axis_index("expert"), lax.axis_index("tensor")
    xl, z = t // nz, lax.rem(t, nz)
    width, tokens = tg.shape
    top = routes.shape[0]
    fc, bins = gate_pre.shape
    half = fc * nz
    rest = width - LANES
    groups = LANES // rest
    rows_g = CAP // groups
    mine = pl.ds(pl.multiple_of(xl * half, LANES), half)
    theirs = pl.ds(pl.multiple_of((1 - xl) * half, LANES), half)

    def chunk(k):
        return lax.rem(z + k + 2 * nz, nz)

    above = (e, xl * nz + chunk(1))
    below = (e, xl * nz + chunk(-1))
    across = (e, (1 - xl) * nz + z)

    def partner(i):
        rel, de = lax.rem(i, 2), i // 2
        pe = lax.rem(e + de, ne)
        return rel, pe, (pe, lax.rem(xl + rel, 2) * nz + z)

    local = [
        pltpu.make_async_copy(src, dst, ls.at[i])
        for i, (src, dst) in enumerate((
            (gate_pre, gate_all.at[z]), (up_pre, up_all.at[z]), (down_w.at[:, mine], down_m),
            (bin_in_h, bin_in), (gate_w.at[:, mine], gate_m), (up_w.at[:, mine], up_m),
        ))
    ]
    for copy in local:
        copy.start()

    barrier = pltpu.get_barrier_semaphore()

    def greet(i, _):
        _, _, device = partner(i)
        pl.semaphore_signal(barrier, inc=1, device_id=device, device_id_type=MESH)
        return 0

    for device in (above, below):
        pl.semaphore_signal(barrier, inc=1, device_id=device, device_id_type=MESH)
    lax.fori_loop(1, 2 * ne, greet, 0)

    expert_ids = lax.broadcasted_iota(jnp.int32, (ne, tokens), 0)
    named = jnp.zeros((ne, tokens), F32)
    weight = jnp.zeros((ne, tokens), F32)
    for k in range(top):
        hit = routes[k : k + 1, :] == expert_ids
        named = named + jnp.where(hit, 1.0, 0.0)
        weight = weight + jnp.where(hit, combine[k : k + 1, :], 0.0)
    before = lax.broadcasted_iota(jnp.int32, (tokens, tokens), 0) < lax.broadcasted_iota(
        jnp.int32, (tokens, tokens), 1
    )
    earlier = nn(named.astype(BF16), jnp.where(before, 1.0, 0.0).astype(BF16))
    slot = jnp.where(named > 0.5, earlier, -1.0)
    slot_ids = lax.broadcasted_iota(jnp.int32, (CAP, tokens), 0).astype(F32)
    for x in range(ne):
        hit = slot_ids == slot[x : x + 1, :]
        place[x] = jnp.where(hit, 1.0, 0.0)
        w = jnp.where(hit, weight[x : x + 1, :], 0.0)
        hi = w.astype(BF16)
        w = w - hi.astype(F32)
        mid = w.astype(BF16)
        split[0, x] = hi
        split[1, x] = mid
        split[2, x] = (w - mid.astype(F32)).astype(BF16)
    tail_t[...] = jnp.zeros_like(tail_t)
    for j in range(groups):
        tail_t[j * rest : (j + 1) * rest, j * tokens : (j + 1) * tokens] = tg[LANES:width, :]
    head, tail = 0.0, 0.0
    for k in range(3):
        head += nt(split[k].reshape(ne * CAP, tokens), tg[0:LANES, :])
        packed = jnp.concatenate(
            [split[k, :, j * rows_g : (j + 1) * rows_g, :].reshape(ne * rows_g, tokens) for j in range(groups)],
            axis=1,
        )
        tail += nt(packed, tail_t[...])
    placed[:, 0:CAP, :] = head.astype(BF16).reshape(ne, CAP, LANES)
    placed[:, CAP:, :] = tail.astype(BF16).reshape(ne, rows_g, LANES)

    pl.semaphore_wait(barrier, 2 * ne + 1)

    sends, due = [], {}

    def start(key, copy):
        copy.start()
        sends.append(copy)
        due[key] = copy

    def hop(ring, s, upward, src, dst):
        start((ring, s, upward), pltpu.make_async_remote_copy(
            src_ref=src, dst_ref=dst,
            send_sem=(su if upward else sd).at[ring, s],
            recv_sem=(ru if upward else rd).at[ring, s],
            device_id=above if upward else below, device_id_type=MESH,
        ))

    def exchange(key, src, dst, send_sem, recv_sem):
        start(key, pltpu.make_async_remote_copy(
            src_ref=src, dst_ref=dst, send_sem=send_sem, recv_sem=recv_sem,
            device_id=across, device_id_type=MESH,
        ))

    def landed(key):
        due.pop(key).wait_recv()

    bulk = {}

    def to_all(key, src, dst, send_sem, recv_sem, only=None):
        def one(i, _):
            rel, pe, device = partner(i if only is None else 2 * i + only)
            pltpu.make_async_remote_copy(
                src_ref=src(rel, pe), dst_ref=dst.at[rel * ne + e],
                send_sem=send_sem, recv_sem=recv_sem, device_id=device, device_id_type=MESH,
            ).start()
            return 0

        first, last = (1, 2 * ne) if only is None else (1 - only, ne)
        lax.fori_loop(first, last, one, 0)
        many = dst.at[pl.ds((only or 0) * ne, last - first)]
        bulk[key] = pltpu.make_async_copy(many, many, recv_sem)
        bulk[key, "sent"] = pltpu.make_async_copy(many, many, send_sem)

    def gather_send(ring, buf, own, s, upward):
        k = chunk(-s if upward else s)
        hop(ring, s, upward, own if s == 0 else buf.at[k], buf.at[k])

    pre_u, pre_d = nz - 1 - nz // 2, nz // 2
    nu, nd = nz // 2, nz - 1 - nz // 2
    progress = [0]

    def pump():
        i = progress[0]
        s, ring = i // 2, i % 2
        if s > pre_d:
            return
        progress[0] += 1
        buf, own = ((gate_all, gate_pre), (up_all, up_pre))[ring]
        for upward, n in ((False, pre_d), (True, pre_u)):
            if 0 < s <= n:
                landed((ring, s - 1, upward))
            if s < n:
                gather_send(ring, buf, own, s, upward)
        if ring == 1 and s > 0:
            if s <= pre_u:
                activate(chunk(-s))
            activate(chunk(s))

    def activate(c):
        def rows(r, _):
            at = pl.ds(pl.multiple_of(r * 16, 16), 16)
            g, u = gate_all[c, at, :].astype(F32), up_all[c, at, :].astype(F32)
            s = 1.0 / (1.0 + jnp.exp(-g))
            a = g * s
            act_up[c, at, :] = a
            act_gate[c, at, :] = u * s * (1.0 + g * (1.0 - s))
            hidden[c, at, :] = (a * u).astype(BF16)
            return 0

        lax.fori_loop(0, fc // 16, rows, 0)

    def deltas(c, h):
        at = halves[h]
        v = total_all[c, :, at].astype(F32)
        up_delta[c, :, at] = (v * act_up[c, :, at]).astype(BF16)
        gate_delta[c, :, at] = (v * act_gate[c, :, at]).astype(BF16)

    halves = [pl.ds(h * (bins // 2), bins // 2) for h in (0, 1)]

    def step(h, i):
        at = halves[h]
        for upward, n, buf, first in ((True, nu, sum_u, first_u), (False, nd, sum_d, first_d)):
            if 0 < i <= n:
                landed((SUM[h], i - 1, upward))
            if i < n:
                c = chunk(nu - i if upward else i - nd)
                if i == 0:
                    first[:, at] = part[c, :, at].astype(BF16)
                else:
                    buf[i - 1, :, at] = (buf[i - 1, :, at].astype(F32) + part[c, :, at]).astype(BF16)
                source = buf.at[i - 1, :, at] if i else first.at[:, at]
                hop(SUM[h], i, upward, source, buf.at[i, :, at])
        if i < nu:
            return
        s = i - nu
        if s == 0:
            total_all[z, :, at] = (
                part[z, :, at] + (sum_u[nu - 1, :, at].astype(F32) + sum_d[nd - 1, :, at].astype(F32))
            ).astype(BF16)
        for upward, n in ((True, nu), (False, nd)):
            if 0 < s <= n:
                landed((ALL[h], s - 1, upward))
            if s < n:
                total = total_all.at[chunk(-s if upward else s), :, at]
                hop(ALL[h], s, upward, total, total)


    def work():
        to_all("out", lambda rel, pe: placed.at[pe], binned, out_s, out_r)
        pump()
        pump()
        exchange("down", down_w.at[:, theirs], down_x, xs.at[0], xr.at[0])
        binned[e] = placed[e]

        pump()
        for i in (0, 1):
            local[i].wait()
        activate(z)
        pump()
        pick[...] = place[...].reshape(ne * CAP, tokens).T.astype(BF16)
        pump()
        local[2].wait()
        down_t[:, 0:LANES] = down_m[0:LANES, :].T
        pump()
        landed("down")
        down_t[:, LANES:] = down_x[0:LANES, :].T
        down_tr[...] = jnp.concatenate([down_m[LANES:, :], down_x[LANES:, :]], axis=0).T
        while progress[0] < EARLY:
            pump()
        bulk.pop("out").wait()

        exchange("in", bin_in_h, in_x, xs.at[1], xr.at[1])
        exchange("gate", gate_w.at[:, theirs], gate_x, xs.at[2], xr.at[2])
        exchange("up", up_w.at[:, theirs], up_x, xs.at[3], xr.at[3])
        for rel in (0, 1):
            for j in range(groups):
                bin_r[:, j * rows_g : (j + 1) * rows_g, rel * rest : (rel + 1) * rest] = binned[
                    rel * ne : (rel + 1) * ne, CAP:, j * rest : (j + 1) * rest
                ]
        heads = [binned[rel * ne : (rel + 1) * ne, 0:CAP, :].reshape(bins, LANES) for rel in (0, 1)]
        part[...] = (
            nt(down_t[...], jnp.concatenate(heads, axis=1))
            + nt(down_tr[...], bin_r[...].reshape(bins, 2 * rest))
        ).reshape(nz, fc, bins)

        step(0, 0)
        for rel in (0, 1):
            bin_t[rel, 0:LANES] = binned[rel * ne : (rel + 1) * ne, 0:CAP, :].reshape(bins, LANES).T
        tails = bin_r[...].reshape(bins, 2 * rest).T
        for rel in (0, 1):
            bin_t[rel, LANES:] = tails[rel * rest : (rel + 1) * rest]
        strips = []
        for slot_no in range(2 * nu + 1 + LAG):
            if 0 < slot_no <= 2 * nu:
                step(0, slot_no)
            if slot_no >= LAG:
                step(1, slot_no - LAG)
            if slot_no % BESIDE == BESIDE - 1:
                pump()
            for h in (0, 1):
                s = slot_no - LAG * h - nu
                if s < 0 or s > nu:
                    continue
                arrived = [0] if s == 0 else [k for k in (-s, s) if -nu <= k <= nd]
                while progress[0] < min(2 * s + 2, 2 * pre_d + 2):
                    pump()
                for k in arrived:
                    deltas(chunk(k), h)
                if h == 0:
                    continue
                if s == 0:
                    local[3].wait()
                    landed("in")
                strips.append(arrived)
                pieces = []
                for k in arrived:
                    pieces += [gate_delta[chunk(k)], up_delta[chunk(k)]]
                n = len(pieces)
                made = nt(jnp.concatenate(pieces, axis=0), in_x[...]).astype(BF16)
                strip[s, 0 : n * fc, :] = made[:, 0:LANES]
                for j in range(n):
                    strip[s, n * fc : (n + 1) * fc, j * rest : (j + 1) * rest] = made[j * fc : (j + 1) * fc, LANES:]
                sent = pl.ds(0, (n + 1) * fc)
                exchange(("strip", s), strip.at[s, sent], strip_in.at[s, sent], ss.at[s], sr.at[s])
                if progress[0] == 2 * pre_d + 2 and "down_grad" not in due:
                    down_s[...] = nt(bin_t[1], hidden[...].reshape(half, bins)).astype(BF16)
                    exchange("down_grad", down_s, down_out.at[:, mine], xs.at[4], xr.at[4])

        gd = gate_delta[...].reshape(half, bins)
        ud = up_delta[...].reshape(half, bins)
        local[4].wait()
        local[5].wait()
        landed("gate")
        landed("up")
        for rel in (1, 0):
            b_t = nn((gate_x if rel else gate_m)[...], gd) + nn((up_x if rel else up_m)[...], ud)
            at = slice(rel * ne, (rel + 1) * ne)
            b_t = b_t.astype(BF16)
            back[at, 0:CAP, :] = b_t[0:LANES].T.reshape(ne, CAP, LANES)
            tail = b_t[LANES:].T.reshape(ne, groups, rows_g, rest)
            for j in range(groups):
                back[at, CAP:, j * rest : (j + 1) * rest] = tail[:, j]
            to_all(("back", rel), lambda rel, pe: back.at[rel * ne + pe], back_in, back_s.at[rel], back_r.at[rel], rel)
        back_in[e] = back[e]

        gate_out[:, mine] = nt(bin_in[...], gd).astype(BF16)
        up_out[:, mine] = nt(bin_in[...], ud).astype(BF16)
        down_out[:, mine] = nt(bin_t[0], hidden[...].reshape(half, bins)).astype(BF16)
        for s, arrived in enumerate(strips):
            landed(("strip", s))
            n = 2 * len(arrived)
            for i, k in enumerate(arrived):
                c = chunk(k)
                for a in (0, 1):
                    j = 2 * i + a
                    grad_t[a, c] = strip_in[s, j * fc : (j + 1) * fc, :]
                    grad_tr[c, :, a * rest : (a + 1) * rest] = strip_in[
                        s, n * fc : (n + 1) * fc, j * rest : (j + 1) * rest
                    ]
        tails = grad_tr[...].reshape(half, 2 * rest).T
        for a, out in enumerate((gate_out, up_out)):
            out[0:LANES, theirs] = grad_t[a].reshape(half, LANES).T
            out[LANES:, theirs] = tails[a * rest : (a + 1) * rest]

        for rel in (1, 0):
            bulk.pop(("back", rel)).wait()
        for rel in (0, 1):
            for j in range(groups):
                tok_r[:, j * rows_g : (j + 1) * rows_g, rel * rest : (rel + 1) * rest] = back_in[
                    rel * ne : (rel + 1) * ne, CAP:, j * rest : (j + 1) * rest
                ]
        token = 0.0
        for rel in (0, 1):
            token += nn(pick[...], back_in[rel * ne : (rel + 1) * ne, 0:CAP, :].reshape(ne * CAP, LANES))
        tok_out[0:LANES, :] = token.T.astype(BF16)
        tail = nn(pick[...], tok_r[...].reshape(ne * CAP, 2 * rest)).T
        tok_out[LANES:, :] = (tail[0:rest] + tail[rest:]).astype(BF16)
        landed("down_grad")

    work()

    for copy in bulk.values():
        copy.wait()
    for copy in sends:
        copy.wait_send()


def finish(*refs):
    n = len(refs) // 3
    ins, outs, held, sems = refs[0:n], refs[n : 2 * n], refs[2 * n : 3 * n], refs[-1]
    reads = [pltpu.make_async_copy(ins[i], held[i], sems.at[i]) for i in range(n)]
    writes = [pltpu.make_async_copy(held[i], outs[i], sems.at[n + i]) for i in range(n)]
    for copy in reads:
        copy.start()
    for i in range(n):
        reads[i].wait()
        writes[i].start()
    for copy in writes:
        copy.wait()


def layer(ne, nz, *args):
    tg, combine, routes, bin_in, gate_pre, up_pre, gate_w, up_w, down_w = args
    bin_in, gate_pre, up_pre, gate_w, up_w, down_w = (
        a.reshape(a.shape[1:]) for a in (bin_in, gate_pre, up_pre, gate_w, up_w, down_w)
    )
    tg, combine, routes, bin_in = tg.T, combine.T, routes.T, bin_in.T
    width, tokens = tg.shape
    fc, bins = gate_pre.shape
    half, ff = fc * nz, gate_w.shape[1]
    nu, nd = nz // 2, nz - 1 - nz // 2
    rest = width - LANES
    groups = LANES // rest
    block = CAP + CAP // groups
    dma = pltpu.SemaphoreType.DMA

    def v(*shape, dtype=BF16):
        return pltpu.VMEM(shape, dtype)

    scratch = [
        v(width, bins), v(width, half), v(width, half), v(width, half),
        v(ne, CAP, tokens, dtype=F32), v(tokens, ne * CAP), v(3, ne, CAP, tokens), v(LANES, groups * tokens),
        v(ne, block, LANES), v(2 * ne, block, LANES), v(ne, CAP, 2 * rest),
        v(2 * ne, block, LANES), v(2 * ne, block, LANES), v(ne, CAP, 2 * rest),
        v(width, half), v(width, half), v(width, half), v(width, bins),
        v(half, 2 * LANES), v(half, 2 * rest), v(2, width, bins), v(nz, fc, bins, dtype=F32),
        v(nu, fc, bins), v(nd, fc, bins), v(fc, bins), v(fc, bins),
        v(nz, fc, bins), v(nz, fc, bins), v(nz, fc, bins),
        v(nz, fc, bins, dtype=F32), v(nz, fc, bins, dtype=F32), v(nz, fc, bins),
        v(nz, fc, bins), v(nz, fc, bins),
        v(width, half), v(nu + 1, 5 * fc, LANES), v(nu + 1, 5 * fc, LANES),
        v(2, nz, fc, LANES), v(nz, fc, 2 * rest),
        dma((6, nu)), dma((6, nu)), dma((6, nu)), dma((6, nu)),
        dma, dma, dma((2,)), dma((2,)), dma((5,)), dma((5,)), dma((nu + 1,)), dma((nu + 1,)), dma((6,)),
    ]
    grad = jax.ShapeDtypeStruct((width, ff), BF16)
    outs = (jax.ShapeDtypeStruct((width, tokens), BF16), grad, grad, grad)
    vmem, hbm = pl.BlockSpec(memory_space=pltpu.VMEM), pl.BlockSpec(memory_space=pl.ANY)
    made = pl.pallas_call(
        functools.partial(kernel, ne, nz),
        out_shape=outs,
        in_specs=[vmem] * 3 + [hbm] * 6,
        out_specs=(vmem,) * 4,
        scratch_shapes=scratch,
        compiler_params=pltpu.CompilerParams(
            collective_id=0, has_side_effects=True, vmem_limit_bytes=58 * 2**20
        ),
        cost_estimate=pl.CostEstimate(
            flops=12 * width * ff * bins, bytes_accessed=6 * 2**20, transcendentals=half * bins
        ),
    )(tg, combine, routes, bin_in, gate_pre, up_pre, gate_w, up_w, down_w)
    made = pl.pallas_call(
        finish,
        out_shape=outs,
        in_specs=[hbm] * 4,
        out_specs=(hbm,) * 4,
        scratch_shapes=[v(width, tokens), v(width, ff), v(width, ff), v(width, ff), dma((8,))],
    )(*made)
    token, gate, up, down = made
    return token.T, gate[None], up[None], down[None]


def solution(mesh):
    ne, nz = mesh.shape["expert"], mesh.shape["tensor"] // 2
    return jax.shard_map(
        functools.partial(layer, ne, nz),
        mesh=mesh,
        in_specs=(
            P("expert", "tensor"),
            P("expert", None),
            P("expert", None),
            P("expert", None, "tensor"),
            P("expert", "tensor", None),
            P("expert", "tensor", None),
            P("expert", "tensor", None),
            P("expert", "tensor", None),
            P("expert", "tensor", None),
        ),
        out_specs=(
            P("expert", "tensor"),
            P("expert", "tensor", None),
            P("expert", "tensor", None),
            P("expert", "tensor", None),
        ),
        check_vma=False,
    )
```

```python
import functools

import jax
import jax.numpy as jnp
from jax import lax
from jax.experimental import pallas as pl
from jax.experimental.pallas import tpu as pltpu
from jax.sharding import PartitionSpec as P

CAP = 64
LANES = 128
F32, BF16 = jnp.float32, jnp.bfloat16
MESH = pl.DeviceIdType.MESH
NT = (((1,), (1,)), ((), ()))

GATE, UP, SUM, ALL = 0, 1, (2, 3), (4, 5)
EARLY, SLOTS = 6, (0, 1) * 4 + (1,) * 9
LAG = 0


def nt(left, right):
    return lax.dot_general(left, right, NT, preferred_element_type=F32)


def nn(left, right):
    return jnp.dot(left, right, preferred_element_type=F32)


def kernel(
    ne, nz,
    tg_h, combine_h, routes_h, bin_in_h, gate_pre, up_pre, gate_w, up_w, down_w,
    tok_out, gate_out, up_out, down_out,
    tg, combine, routes, bin_in, gate_m, up_m, down_m,
    place, pick, split, tail_t, placed, binned, bin_r, back, back_in, tok_r,
    down_x, gate_x, up_x, in_x, down_t, down_tr, bin_w, bin_t, part,
    sum_u, sum_d, first_u, first_d, gate_all, up_all, total_all,
    act_up, act_gate, hidden, gate_delta, up_delta,
    down_s, strip, strip_in, grad_t, grad_tr,
    su, ru, sd, rd, out_s, out_r, back_s, back_r, xs, xr, ss, sr, ls,
):
    e, t = lax.axis_index("expert"), lax.axis_index("tensor")
    xl, z = t // nz, lax.rem(t, nz)
    width, tokens = tg_h.shape
    top = routes_h.shape[0]
    fc, bins = gate_pre.shape
    half = fc * nz
    rest = width - LANES
    groups = LANES // rest
    rows_g = CAP // groups
    mine = pl.ds(pl.multiple_of(xl * half, LANES), half)
    theirs = pl.ds(pl.multiple_of((1 - xl) * half, LANES), half)

    def chunk(k):
        return lax.rem(z + k + 2 * nz, nz)

    above = (e, xl * nz + chunk(1))
    below = (e, xl * nz + chunk(-1))
    across = (e, (1 - xl) * nz + z)

    def partner(i):
        rel, de = lax.rem(i, 2), i // 2
        pe = lax.rem(e + de, ne)
        return rel, pe, (pe, lax.rem(xl + rel, 2) * nz + z)

    local = [
        pltpu.make_async_copy(src, dst, ls.at[i])
        for i, (src, dst) in enumerate((
            (gate_pre, gate_all.at[z]), (up_pre, up_all.at[z]), (down_w.at[:, mine], down_m),
            (bin_in_h, bin_in), (gate_w.at[:, mine], gate_m), (up_w.at[:, mine], up_m),
            (routes_h, routes), (combine_h, combine), (tg_h, tg),
        ))
    ]
    for copy in local[6:] + local[:6]:
        copy.start()

    barrier = pltpu.get_barrier_semaphore()

    def greet(i, _):
        _, _, device = partner(i)
        pl.semaphore_signal(barrier, inc=1, device_id=device, device_id_type=MESH)
        return 0

    for device in (above, below):
        pl.semaphore_signal(barrier, inc=1, device_id=device, device_id_type=MESH)
    lax.fori_loop(1, 2 * ne, greet, 0)

    for copy in local[6:]:
        copy.wait()
    expert_ids = lax.broadcasted_iota(jnp.int32, (ne, tokens), 0)
    named = jnp.zeros((ne, tokens), F32)
    weight = jnp.zeros((ne, tokens), F32)
    for k in range(top):
        hit = routes[k : k + 1, :] == expert_ids
        named = named + jnp.where(hit, 1.0, 0.0)
        weight = weight + jnp.where(hit, combine[k : k + 1, :], 0.0)
    before = lax.broadcasted_iota(jnp.int32, (tokens, tokens), 0) < lax.broadcasted_iota(
        jnp.int32, (tokens, tokens), 1
    )
    earlier = nn(named.astype(BF16), jnp.where(before, 1.0, 0.0).astype(BF16))
    slot = jnp.where(named > 0.5, earlier, -1.0)
    slot_ids = lax.broadcasted_iota(jnp.int32, (CAP, tokens), 0).astype(F32)
    for x in range(ne):
        hit = slot_ids == slot[x : x + 1, :]
        place[x] = jnp.where(hit, 1.0, 0.0)
        w = jnp.where(hit, weight[x : x + 1, :], 0.0)
        hi = w.astype(BF16)
        w = w - hi.astype(F32)
        mid = w.astype(BF16)
        split[0, x] = hi
        split[1, x] = mid
        split[2, x] = (w - mid.astype(F32)).astype(BF16)
    tail_t[...] = jnp.zeros_like(tail_t)
    for j in range(groups):
        tail_t[j * rest : (j + 1) * rest, j * tokens : (j + 1) * tokens] = tg[LANES:width, :]
    head, tail = 0.0, 0.0
    for k in range(3):
        head += nt(split[k].reshape(ne * CAP, tokens), tg[0:LANES, :])
        packed = jnp.concatenate(
            [split[k, :, j * rows_g : (j + 1) * rows_g, :].reshape(ne * rows_g, tokens) for j in range(groups)],
            axis=1,
        )
        tail += nt(packed, tail_t[...])
    placed[:, 0:CAP, :] = head.astype(BF16).reshape(ne, CAP, LANES)
    placed[:, CAP:, :] = tail.astype(BF16).reshape(ne, rows_g, LANES)

    pl.semaphore_wait(barrier, 2 * ne + 1)

    sends, due = [], {}

    def start(key, copy):
        copy.start()
        sends.append(copy)
        due[key] = copy

    def hop(ring, s, upward, src, dst):
        start((ring, s, upward), pltpu.make_async_remote_copy(
            src_ref=src, dst_ref=dst,
            send_sem=(su if upward else sd).at[ring, s],
            recv_sem=(ru if upward else rd).at[ring, s],
            device_id=above if upward else below, device_id_type=MESH,
        ))

    def exchange(key, src, dst, send_sem, recv_sem):
        start(key, pltpu.make_async_remote_copy(
            src_ref=src, dst_ref=dst, send_sem=send_sem, recv_sem=recv_sem,
            device_id=across, device_id_type=MESH,
        ))

    def landed(key):
        due.pop(key).wait_recv()

    bulk = {}

    def to_all(key, src, dst, send_sem, recv_sem, only=None):
        def one(i, _):
            rel, pe, device = partner(i if only is None else 2 * i + only)
            pltpu.make_async_remote_copy(
                src_ref=src(rel, pe), dst_ref=dst.at[rel * ne + e],
                send_sem=send_sem, recv_sem=recv_sem, device_id=device, device_id_type=MESH,
            ).start()
            return 0

        first, last = (1, 2 * ne) if only is None else (1 - only, ne)
        lax.fori_loop(first, last, one, 0)
        many = dst.at[pl.ds((only or 0) * ne, last - first)]
        bulk[key] = pltpu.make_async_copy(many, many, recv_sem)
        bulk[key, "sent"] = pltpu.make_async_copy(many, many, send_sem)

    def gather_send(ring, buf, own, s, upward):
        k = chunk(-s if upward else s)
        hop(ring, s, upward, own if s == 0 else buf.at[k], buf.at[k])

    pre_u, pre_d = nz - 1 - nz // 2, nz // 2
    nu, nd = nz // 2, nz - 1 - nz // 2
    progress = [0]

    def pump():
        i = progress[0]
        s, ring = i // 2, i % 2
        if s > pre_d:
            return
        progress[0] += 1
        buf, own = ((gate_all, gate_pre), (up_all, up_pre))[ring]
        for upward, n in ((False, pre_d), (True, pre_u)):
            if 0 < s <= n:
                landed((ring, s - 1, upward))
            if s < n:
                gather_send(ring, buf, own, s, upward)
        if ring == 1 and s > 0:
            if s <= pre_u:
                activate(chunk(-s))
            activate(chunk(s))

    def activate(c):
        def rows(r, _):
            at = pl.ds(pl.multiple_of(r * 16, 16), 16)
            g, u = gate_all[c, at, :].astype(F32), up_all[c, at, :].astype(F32)
            s = 1.0 / (1.0 + jnp.exp(-g))
            a = g * s
            act_up[c, at, :] = a
            act_gate[c, at, :] = u * s * (1.0 + g * (1.0 - s))
            hidden[c, at, :] = (a * u).astype(BF16)
            return 0

        lax.fori_loop(0, fc // 16, rows, 0)

    def deltas(c, h):
        at = halves[h]
        v = total_all[c, :, at].astype(F32)
        up_delta[c, :, at] = (v * act_up[c, :, at]).astype(BF16)
        gate_delta[c, :, at] = (v * act_gate[c, :, at]).astype(BF16)

    halves = [pl.ds(h * (bins // 2), bins // 2) for h in (0, 1)]

    def step(h, i):
        at = halves[h]
        for upward, n, buf, first in ((True, nu, sum_u, first_u), (False, nd, sum_d, first_d)):
            if 0 < i <= n:
                landed((SUM[h], i - 1, upward))
            if i < n:
                c = chunk(nu - i if upward else i - nd)
                if i == 0:
                    first[:, at] = part[c, :, at].astype(BF16)
                else:
                    buf[i - 1, :, at] = (buf[i - 1, :, at].astype(F32) + part[c, :, at]).astype(BF16)
                source = buf.at[i - 1, :, at] if i else first.at[:, at]
                hop(SUM[h], i, upward, source, buf.at[i, :, at])
        if i < nu:
            return
        s = i - nu
        if s == 0:
            total_all[z, :, at] = (
                part[z, :, at] + (sum_u[nu - 1, :, at].astype(F32) + sum_d[nd - 1, :, at].astype(F32))
            ).astype(BF16)
        for upward, n in ((True, nu), (False, nd)):
            if 0 < s <= n:
                landed((ALL[h], s - 1, upward))
            if s < n:
                total = total_all.at[chunk(-s if upward else s), :, at]
                hop(ALL[h], s, upward, total, total)


    def work():
        to_all("out", lambda rel, pe: placed.at[pe], binned, out_s, out_r)
        pump()
        pump()
        exchange("down", down_w.at[:, theirs], down_x, xs.at[0], xr.at[0])
        binned[e] = placed[e]

        pump()
        for i in (0, 1):
            local[i].wait()
        activate(z)
        pump()
        pick[...] = place[...].reshape(ne * CAP, tokens).T.astype(BF16)
        pump()
        local[2].wait()
        down_t[:, 0:LANES] = down_m[0:LANES, :].T
        pump()
        landed("down")
        down_t[:, LANES:] = down_x[0:LANES, :].T
        down_tr[...] = jnp.concatenate([down_m[LANES:, :], down_x[LANES:, :]], axis=0).T
        while progress[0] < EARLY:
            pump()
        bulk.pop("out").wait()

        exchange("in", bin_in_h, in_x, xs.at[1], xr.at[1])
        exchange("gate", gate_w.at[:, theirs], gate_x, xs.at[2], xr.at[2])
        exchange("up", up_w.at[:, theirs], up_x, xs.at[3], xr.at[3])
        for rel in (0, 1):
            for j in range(groups):
                bin_r[:, j * rows_g : (j + 1) * rows_g, rel * rest : (rel + 1) * rest] = binned[
                    rel * ne : (rel + 1) * ne, CAP:, j * rest : (j + 1) * rest
                ]
        for rel in (0, 1):
            bin_w[:, rel * LANES : (rel + 1) * LANES] = binned[rel * ne : (rel + 1) * ne, 0:CAP, :].reshape(bins, LANES)

        def products(ks):
            at = [pl.ds(pl.multiple_of(chunk(k) * fc, 16), fc) for k in ks]
            made = nt(jnp.concatenate([down_t[a, :] for a in at], axis=0), bin_w[...]) + nt(
                jnp.concatenate([down_tr[a, :] for a in at], axis=0), bin_r[...].reshape(bins, 2 * rest)
            )
            for i, k in enumerate(ks):
                part[chunk(k)] = made[i * fc : (i + 1) * fc]

        products([nu, -nd])

        step(0, 0)
        for rel in (0, 1):
            bin_t[rel, 0:LANES] = binned[rel * ne : (rel + 1) * ne, 0:CAP, :].reshape(bins, LANES).T
        tails = bin_r[...].reshape(bins, 2 * rest).T
        for rel in (0, 1):
            bin_t[rel, LANES:] = tails[rel * rest : (rel + 1) * rest]
        strips = []
        for slot_no in range(2 * nu + 1 + LAG):
            if 0 < slot_no <= nu:
                products([k for k in (nu - slot_no, slot_no - nd) if k > 0 or slot_no < nd] if slot_no < nu else [0])
            if 0 < slot_no <= 2 * nu:
                step(0, slot_no)
            if slot_no >= LAG:
                step(1, slot_no - LAG)
            for _ in range(SLOTS[slot_no]):
                pump()
            for h in (0, 1):
                s = slot_no - LAG * h - nu
                if s < 0 or s > nu:
                    continue
                arrived = [0] if s == 0 else [k for k in (-s, s) if -nu <= k <= nd]
                while progress[0] < min(2 * s + 2, 2 * pre_d + 2):
                    pump()
                for k in arrived:
                    deltas(chunk(k), h)
                if h == 0:
                    continue
                if s == 0:
                    local[3].wait()
                    landed("in")
                strips.append(arrived)
                pieces = []
                for k in arrived:
                    pieces += [gate_delta[chunk(k)], up_delta[chunk(k)]]
                n = len(pieces)
                made = nt(jnp.concatenate(pieces, axis=0), in_x[...]).astype(BF16)
                strip[s, 0 : n * fc, :] = made[:, 0:LANES]
                for j in range(n):
                    strip[s, n * fc : (n + 1) * fc, j * rest : (j + 1) * rest] = made[j * fc : (j + 1) * fc, LANES:]
                sent = pl.ds(0, (n + 1) * fc)
                exchange(("strip", s), strip.at[s, sent], strip_in.at[s, sent], ss.at[s], sr.at[s])
                if progress[0] == 2 * pre_d + 2 and "down_grad" not in due:
                    down_s[...] = nt(bin_t[1], hidden[...].reshape(half, bins)).astype(BF16)
                    exchange("down_grad", down_s, down_out.at[:, mine], xs.at[4], xr.at[4])

        gd = gate_delta[...].reshape(half, bins)
        ud = up_delta[...].reshape(half, bins)
        local[4].wait()
        local[5].wait()
        landed("gate")
        landed("up")
        for rel in (1, 0):
            b_t = nn((gate_x if rel else gate_m)[...], gd) + nn((up_x if rel else up_m)[...], ud)
            at = slice(rel * ne, (rel + 1) * ne)
            b_t = b_t.astype(BF16)
            back[at, 0:CAP, :] = b_t[0:LANES].T.reshape(ne, CAP, LANES)
            tail = b_t[LANES:].T.reshape(ne, groups, rows_g, rest)
            for j in range(groups):
                back[at, CAP:, j * rest : (j + 1) * rest] = tail[:, j]
            to_all(("back", rel), lambda rel, pe: back.at[rel * ne + pe], back_in, back_s.at[rel], back_r.at[rel], rel)
        back_in[e] = back[e]

        gate_out[:, mine] = nt(bin_in[...], gd).astype(BF16)
        up_out[:, mine] = nt(bin_in[...], ud).astype(BF16)
        down_out[:, mine] = nt(bin_t[0], hidden[...].reshape(half, bins)).astype(BF16)
        for s, arrived in enumerate(strips):
            landed(("strip", s))
            n = 2 * len(arrived)
            for i, k in enumerate(arrived):
                c = chunk(k)
                for a in (0, 1):
                    j = 2 * i + a
                    grad_t[a, c] = strip_in[s, j * fc : (j + 1) * fc, :]
                    grad_tr[c, :, a * rest : (a + 1) * rest] = strip_in[
                        s, n * fc : (n + 1) * fc, j * rest : (j + 1) * rest
                    ]
        tails = grad_tr[...].reshape(half, 2 * rest).T
        for a, out in enumerate((gate_out, up_out)):
            out[0:LANES, theirs] = grad_t[a].reshape(half, LANES).T
            out[LANES:, theirs] = tails[a * rest : (a + 1) * rest]

        for rel in (1, 0):
            bulk.pop(("back", rel)).wait()
        for rel in (0, 1):
            for j in range(groups):
                tok_r[:, j * rows_g : (j + 1) * rows_g, rel * rest : (rel + 1) * rest] = back_in[
                    rel * ne : (rel + 1) * ne, CAP:, j * rest : (j + 1) * rest
                ]
        token = 0.0
        for rel in (0, 1):
            token += nn(pick[...], back_in[rel * ne : (rel + 1) * ne, 0:CAP, :].reshape(ne * CAP, LANES))
        tok_out[0:LANES, :] = token.T.astype(BF16)
        tail = nn(pick[...], tok_r[...].reshape(ne * CAP, 2 * rest)).T
        tok_out[LANES:, :] = (tail[0:rest] + tail[rest:]).astype(BF16)
        landed("down_grad")

    work()

    for copy in bulk.values():
        copy.wait()
    for copy in sends:
        copy.wait_send()


def finish(*refs):
    n = len(refs) // 3
    ins, outs, held, sems = refs[0:n], refs[n : 2 * n], refs[2 * n : 3 * n], refs[-1]
    reads = [pltpu.make_async_copy(ins[i], held[i], sems.at[i]) for i in range(n)]
    writes = [pltpu.make_async_copy(held[i], outs[i], sems.at[n + i]) for i in range(n)]
    for copy in reads:
        copy.start()
    for i in range(n):
        reads[i].wait()
        writes[i].start()
    for copy in writes:
        copy.wait()


def layer(ne, nz, *args):
    tg, combine, routes, bin_in, gate_pre, up_pre, gate_w, up_w, down_w = args
    bin_in, gate_pre, up_pre, gate_w, up_w, down_w = (
        a.reshape(a.shape[1:]) for a in (bin_in, gate_pre, up_pre, gate_w, up_w, down_w)
    )
    tg, combine, routes, bin_in = tg.T, combine.T, routes.T, bin_in.T
    width, tokens = tg.shape
    fc, bins = gate_pre.shape
    half, ff = fc * nz, gate_w.shape[1]
    nu, nd = nz // 2, nz - 1 - nz // 2
    rest = width - LANES
    groups = LANES // rest
    block = CAP + CAP // groups
    dma = pltpu.SemaphoreType.DMA

    def v(*shape, dtype=BF16):
        return pltpu.VMEM(shape, dtype)

    scratch = [
        v(*tg.shape), v(*combine.shape, dtype=F32), v(*routes.shape, dtype=jnp.int32),
        v(width, bins), v(width, half), v(width, half), v(width, half),
        v(ne, CAP, tokens, dtype=F32), v(tokens, ne * CAP), v(3, ne, CAP, tokens), v(LANES, groups * tokens),
        v(ne, block, LANES), v(2 * ne, block, LANES), v(ne, CAP, 2 * rest),
        v(2 * ne, block, LANES), v(2 * ne, block, LANES), v(ne, CAP, 2 * rest),
        v(width, half), v(width, half), v(width, half), v(width, bins),
        v(half, 2 * LANES), v(half, 2 * rest), v(bins, 2 * LANES), v(2, width, bins), v(nz, fc, bins, dtype=F32),
        v(nu, fc, bins), v(nd, fc, bins), v(fc, bins), v(fc, bins),
        v(nz, fc, bins), v(nz, fc, bins), v(nz, fc, bins),
        v(nz, fc, bins, dtype=F32), v(nz, fc, bins, dtype=F32), v(nz, fc, bins),
        v(nz, fc, bins), v(nz, fc, bins),
        v(width, half), v(nu + 1, 5 * fc, LANES), v(nu + 1, 5 * fc, LANES),
        v(2, nz, fc, LANES), v(nz, fc, 2 * rest),
        dma((6, nu)), dma((6, nu)), dma((6, nu)), dma((6, nu)),
        dma, dma, dma((2,)), dma((2,)), dma((5,)), dma((5,)), dma((nu + 1,)), dma((nu + 1,)), dma((9,)),
    ]
    grad = jax.ShapeDtypeStruct((width, ff), BF16)
    outs = (jax.ShapeDtypeStruct((width, tokens), BF16), grad, grad, grad)
    vmem, hbm = pl.BlockSpec(memory_space=pltpu.VMEM), pl.BlockSpec(memory_space=pl.ANY)
    made = pl.pallas_call(
        functools.partial(kernel, ne, nz),
        out_shape=outs,
        in_specs=[pl.BlockSpec(memory_space=pltpu.HBM)] * 9,
        out_specs=(vmem,) * 4,
        scratch_shapes=scratch,
        compiler_params=pltpu.CompilerParams(
            collective_id=0, has_side_effects=True, vmem_limit_bytes=58 * 2**20
        ),
        cost_estimate=pl.CostEstimate(
            flops=12 * width * ff * bins, bytes_accessed=6 * 2**20, transcendentals=half * bins
        ),
    )(tg, combine, routes, bin_in, gate_pre, up_pre, gate_w, up_w, down_w)
    made = pl.pallas_call(
        finish,
        out_shape=outs,
        in_specs=[hbm] * 4,
        out_specs=(hbm,) * 4,
        scratch_shapes=[v(width, tokens), v(width, ff), v(width, ff), v(width, ff), dma((8,))],
    )(*made)
    token, gate, up, down = made
    return token.T, gate[None], up[None], down[None]


def solution(mesh):
    ne, nz = mesh.shape["expert"], mesh.shape["tensor"] // 2
    return jax.shard_map(
        functools.partial(layer, ne, nz),
        mesh=mesh,
        in_specs=(
            P("expert", "tensor"),
            P("expert", None),
            P("expert", None),
            P("expert", None, "tensor"),
            P("expert", "tensor", None),
            P("expert", "tensor", None),
            P("expert", "tensor", None),
            P("expert", "tensor", None),
            P("expert", "tensor", None),
        ),
        out_specs=(
            P("expert", "tensor"),
            P("expert", "tensor", None),
            P("expert", "tensor", None),
            P("expert", "tensor", None),
        ),
        check_vma=False,
    )
```

```python
import functools

import jax
import jax.numpy as jnp
from jax import lax
from jax.experimental import pallas as pl
from jax.experimental.pallas import tpu as pltpu
from jax.sharding import PartitionSpec as P

CAP = 64
LANES = 128
F32, BF16 = jnp.float32, jnp.bfloat16
MESH = pl.DeviceIdType.MESH
NT = (((1,), (1,)), ((), ()))

GATE, UP, SUM, ALL = 0, 1, (2, 3), (4, 5)
EARLY, SLOTS = 6, (0, 1) * 4 + (1,) * 9
LAG = 0


def nt(left, right):
    return lax.dot_general(left, right, NT, preferred_element_type=F32)


def nn(left, right):
    return jnp.dot(left, right, preferred_element_type=F32)


def kernel(
    ne, nz,
    tg_h, combine_h, routes_h, bin_in_h, gate_pre, up_pre, gate_w, up_w, down_w,
    tok_out, gate_out, up_out, down_out,
    tg, combine, routes, bin_in, gate_m, up_m, down_m,
    place, pick, split, tail_t, placed, binned, bin_r, back, back_in, tok_r,
    down_x, gate_x, up_x, in_x, down_t, down_tr, bin_w, bin_t, part,
    sum_u, sum_d, first_u, first_d, gate_all, up_all, total_all,
    act_up, act_gate, hidden, gate_delta, up_delta,
    down_s, strip, strip_in, grad_t, grad_tr,
    su, ru, sd, rd, out_s, out_r, back_s, back_r, xs, xr, ss, sr, ls,
):
    e, t = lax.axis_index("expert"), lax.axis_index("tensor")
    xl, z = t // nz, lax.rem(t, nz)
    width, tokens = tg_h.shape
    top = routes_h.shape[0]
    fc, bins = gate_pre.shape
    half = fc * nz
    rest = width - LANES
    groups = LANES // rest
    rows_g = CAP // groups
    mine = pl.ds(pl.multiple_of(xl * half, LANES), half)
    theirs = pl.ds(pl.multiple_of((1 - xl) * half, LANES), half)

    def chunk(k):
        return lax.rem(z + k + 2 * nz, nz)

    above = (e, xl * nz + chunk(1))
    below = (e, xl * nz + chunk(-1))
    across = (e, (1 - xl) * nz + z)

    def partner(i):
        rel, de = lax.rem(i, 2), i // 2
        pe = lax.rem(e + de, ne)
        return rel, pe, (pe, lax.rem(xl + rel, 2) * nz + z)

    local = [
        pltpu.make_async_copy(src, dst, ls.at[i])
        for i, (src, dst) in enumerate((
            (gate_pre, gate_all.at[z]), (up_pre, up_all.at[z]), (down_w.at[:, mine], down_m),
            (bin_in_h, bin_in), (gate_w.at[:, mine], gate_m), (up_w.at[:, mine], up_m),
            (routes_h, routes), (combine_h, combine), (tg_h, tg),
        ))
    ]
    for copy in local[6:] + local[:6]:
        copy.start()

    barrier = pltpu.get_barrier_semaphore()

    def greet(i, _):
        _, _, device = partner(i)
        pl.semaphore_signal(barrier, inc=1, device_id=device, device_id_type=MESH)
        return 0

    for device in (above, below):
        pl.semaphore_signal(barrier, inc=1, device_id=device, device_id_type=MESH)
    lax.fori_loop(1, 2 * ne, greet, 0)

    for copy in local[6:]:
        copy.wait()
    expert_ids = lax.broadcasted_iota(jnp.int32, (ne, tokens), 0)
    named = jnp.zeros((ne, tokens), F32)
    weight = jnp.zeros((ne, tokens), F32)
    for k in range(top):
        hit = routes[k : k + 1, :] == expert_ids
        named = named + jnp.where(hit, 1.0, 0.0)
        weight = weight + jnp.where(hit, combine[k : k + 1, :], 0.0)
    before = lax.broadcasted_iota(jnp.int32, (tokens, tokens), 0) < lax.broadcasted_iota(
        jnp.int32, (tokens, tokens), 1
    )
    earlier = nn(named.astype(BF16), jnp.where(before, 1.0, 0.0).astype(BF16))
    slot = jnp.where(named > 0.5, earlier, -1.0)
    slot_ids = lax.broadcasted_iota(jnp.int32, (CAP, tokens), 0).astype(F32)
    for x in range(ne):
        hit = slot_ids == slot[x : x + 1, :]
        place[x] = jnp.where(hit, 1.0, 0.0)
        w = jnp.where(hit, weight[x : x + 1, :], 0.0)
        hi = w.astype(BF16)
        w = w - hi.astype(F32)
        mid = w.astype(BF16)
        split[0, x] = hi
        split[1, x] = mid
        split[2, x] = (w - mid.astype(F32)).astype(BF16)
    tail_t[...] = jnp.zeros_like(tail_t)
    for j in range(groups):
        tail_t[j * rest : (j + 1) * rest, j * tokens : (j + 1) * tokens] = tg[LANES:width, :]
    head, tail = 0.0, 0.0
    for k in range(3):
        head += nt(split[k].reshape(ne * CAP, tokens), tg[0:LANES, :])
        packed = jnp.concatenate(
            [split[k, :, j * rows_g : (j + 1) * rows_g, :].reshape(ne * rows_g, tokens) for j in range(groups)],
            axis=1,
        )
        tail += nt(packed, tail_t[...])
    placed[:, 0:CAP, :] = head.astype(BF16).reshape(ne, CAP, LANES)
    placed[:, CAP:, :] = tail.astype(BF16).reshape(ne, rows_g, LANES)

    pl.semaphore_wait(barrier, 2 * ne + 1)

    sends, due = [], {}

    def start(key, copy):
        copy.start()
        sends.append(copy)
        due[key] = copy

    def hop(ring, s, upward, src, dst):
        start((ring, s, upward), pltpu.make_async_remote_copy(
            src_ref=src, dst_ref=dst,
            send_sem=(su if upward else sd).at[ring, s],
            recv_sem=(ru if upward else rd).at[ring, s],
            device_id=above if upward else below, device_id_type=MESH,
        ))

    def exchange(key, src, dst, send_sem, recv_sem):
        start(key, pltpu.make_async_remote_copy(
            src_ref=src, dst_ref=dst, send_sem=send_sem, recv_sem=recv_sem,
            device_id=across, device_id_type=MESH,
        ))

    def landed(key):
        due.pop(key).wait_recv()

    bulk = {}

    def to_all(key, src, dst, send_sem, recv_sem, only=None):
        def one(i, _):
            if only is None:
                i = lax.rem(i + ne - 1, 2 * ne - 1) + 1
            elif only == 0:
                i = 2 * (lax.rem(i + ne // 2 - 2, ne - 1) + 1)
            else:
                i = 2 * lax.rem(i + ne // 2, ne) + 1
            rel, pe, device = partner(i)
            pltpu.make_async_remote_copy(
                src_ref=src(rel, pe), dst_ref=dst.at[rel * ne + e],
                send_sem=send_sem, recv_sem=recv_sem, device_id=device, device_id_type=MESH,
            ).start()
            return 0

        first, last = (1, 2 * ne) if only is None else (1 - only, ne)
        lax.fori_loop(first, last, one, 0)
        many = dst.at[pl.ds((only or 0) * ne, last - first)]
        bulk[key] = pltpu.make_async_copy(many, many, recv_sem)
        bulk[key, "sent"] = pltpu.make_async_copy(many, many, send_sem)

    def gather_send(ring, buf, own, s, upward):
        k = chunk(-s if upward else s)
        hop(ring, s, upward, own if s == 0 else buf.at[k], buf.at[k])

    pre_u, pre_d = nz - 1 - nz // 2, nz // 2
    nu, nd = nz // 2, nz - 1 - nz // 2
    progress = [0]

    def pump():
        i = progress[0]
        s, ring = i // 2, i % 2
        if s > pre_d:
            return
        progress[0] += 1
        buf, own = ((gate_all, gate_pre), (up_all, up_pre))[ring]
        for upward, n in ((False, pre_d), (True, pre_u)):
            if 0 < s <= n:
                landed((ring, s - 1, upward))
            if s < n:
                gather_send(ring, buf, own, s, upward)
        if ring == 1 and s > 0:
            if s <= pre_u:
                activate(chunk(-s))
            activate(chunk(s))

    def activate(c):
        def rows(r, _):
            at = pl.ds(pl.multiple_of(r * 16, 16), 16)
            g, u = gate_all[c, at, :].astype(F32), up_all[c, at, :].astype(F32)
            s = 1.0 / (1.0 + jnp.exp(-g))
            a = g * s
            act_up[c, at, :] = a
            act_gate[c, at, :] = u * s * (1.0 + g * (1.0 - s))
            hidden[c, at, :] = (a * u).astype(BF16)
            return 0

        lax.fori_loop(0, fc // 16, rows, 0)

    def deltas(c, h):
        at = halves[h]
        v = total_all[c, :, at].astype(F32)
        up_delta[c, :, at] = (v * act_up[c, :, at]).astype(BF16)
        gate_delta[c, :, at] = (v * act_gate[c, :, at]).astype(BF16)

    halves = [pl.ds(h * (bins // 2), bins // 2) for h in (0, 1)]

    def step(h, i):
        at = halves[h]
        for upward, n, buf, first in ((True, nu, sum_u, first_u), (False, nd, sum_d, first_d)):
            if 0 < i <= n:
                landed((SUM[h], i - 1, upward))
            if i < n:
                c = chunk(nu - i if upward else i - nd)
                if i == 0:
                    first[:, at] = part[c, :, at].astype(BF16)
                else:
                    buf[i - 1, :, at] = (buf[i - 1, :, at].astype(F32) + part[c, :, at]).astype(BF16)
                source = buf.at[i - 1, :, at] if i else first.at[:, at]
                hop(SUM[h], i, upward, source, buf.at[i, :, at])
        if i < nu:
            return
        s = i - nu
        if s == 0:
            total_all[z, :, at] = (
                part[z, :, at] + (sum_u[nu - 1, :, at].astype(F32) + sum_d[nd - 1, :, at].astype(F32))
            ).astype(BF16)
        for upward, n in ((True, nu), (False, nd)):
            if 0 < s <= n:
                landed((ALL[h], s - 1, upward))
            if s < n:
                total = total_all.at[chunk(-s if upward else s), :, at]
                hop(ALL[h], s, upward, total, total)


    def work():
        pump()
        pump()
        to_all("out", lambda rel, pe: placed.at[pe], binned, out_s, out_r)
        exchange("down", down_w.at[:, theirs], down_x, xs.at[0], xr.at[0])
        binned[e] = placed[e]

        pump()
        for i in (0, 1):
            local[i].wait()
        activate(z)
        pump()
        pick[...] = place[...].reshape(ne * CAP, tokens).T.astype(BF16)
        pump()
        local[2].wait()
        down_t[:, 0:LANES] = down_m[0:LANES, :].T
        pump()
        landed("down")
        down_t[:, LANES:] = down_x[0:LANES, :].T
        down_tr[...] = jnp.concatenate([down_m[LANES:, :], down_x[LANES:, :]], axis=0).T
        while progress[0] < EARLY:
            pump()
        bulk.pop("out").wait()

        exchange("in", bin_in_h, in_x, xs.at[1], xr.at[1])
        exchange("gate", gate_w.at[:, theirs], gate_x, xs.at[2], xr.at[2])
        exchange("up", up_w.at[:, theirs], up_x, xs.at[3], xr.at[3])
        for rel in (0, 1):
            for j in range(groups):
                bin_r[:, j * rows_g : (j + 1) * rows_g, rel * rest : (rel + 1) * rest] = binned[
                    rel * ne : (rel + 1) * ne, CAP:, j * rest : (j + 1) * rest
                ]
        for rel in (0, 1):
            bin_w[:, rel * LANES : (rel + 1) * LANES] = binned[rel * ne : (rel + 1) * ne, 0:CAP, :].reshape(bins, LANES)

        def products(ks):
            at = [pl.ds(pl.multiple_of(chunk(k) * fc, 16), fc) for k in ks]
            made = nt(jnp.concatenate([down_t[a, :] for a in at], axis=0), bin_w[...]) + nt(
                jnp.concatenate([down_tr[a, :] for a in at], axis=0), bin_r[...].reshape(bins, 2 * rest)
            )
            for i, k in enumerate(ks):
                part[chunk(k)] = made[i * fc : (i + 1) * fc]

        products([nu, -nd])

        step(0, 0)
        for rel in (0, 1):
            bin_t[rel, 0:LANES] = binned[rel * ne : (rel + 1) * ne, 0:CAP, :].reshape(bins, LANES).T
        tails = bin_r[...].reshape(bins, 2 * rest).T
        for rel in (0, 1):
            bin_t[rel, LANES:] = tails[rel * rest : (rel + 1) * rest]
        strips = []
        for slot_no in range(2 * nu + 1 + LAG):
            if 0 < slot_no <= nu:
                products([k for k in (nu - slot_no, slot_no - nd) if k > 0 or slot_no < nd] if slot_no < nu else [0])
            if 0 < slot_no <= 2 * nu:
                step(0, slot_no)
            if slot_no >= LAG:
                step(1, slot_no - LAG)
            for _ in range(SLOTS[slot_no]):
                pump()
            for h in (0, 1):
                s = slot_no - LAG * h - nu
                if s < 0 or s > nu:
                    continue
                arrived = [0] if s == 0 else [k for k in (-s, s) if -nu <= k <= nd]
                while progress[0] < min(2 * s + 2, 2 * pre_d + 2):
                    pump()
                for k in arrived:
                    deltas(chunk(k), h)
                if h == 0:
                    continue
                if s == 0:
                    local[3].wait()
                    landed("in")
                strips.append(arrived)
                pieces = []
                for k in arrived:
                    pieces += [gate_delta[chunk(k)], up_delta[chunk(k)]]
                n = len(pieces)
                made = nt(jnp.concatenate(pieces, axis=0), in_x[...]).astype(BF16)
                strip[s, 0 : n * fc, :] = made[:, 0:LANES]
                for j in range(n):
                    strip[s, n * fc : (n + 1) * fc, j * rest : (j + 1) * rest] = made[j * fc : (j + 1) * fc, LANES:]
                sent = pl.ds(0, (n + 1) * fc)
                exchange(("strip", s), strip.at[s, sent], strip_in.at[s, sent], ss.at[s], sr.at[s])
                if progress[0] == 2 * pre_d + 2 and "down_grad" not in due:
                    down_s[...] = nt(bin_t[1], hidden[...].reshape(half, bins)).astype(BF16)
                    exchange("down_grad", down_s, down_out.at[:, mine], xs.at[4], xr.at[4])

        gd = gate_delta[...].reshape(half, bins)
        ud = up_delta[...].reshape(half, bins)
        local[4].wait()
        local[5].wait()
        landed("gate")
        landed("up")
        for rel in (1, 0):
            b_t = nn((gate_x if rel else gate_m)[...], gd) + nn((up_x if rel else up_m)[...], ud)
            at = slice(rel * ne, (rel + 1) * ne)
            b_t = b_t.astype(BF16)
            back[at, 0:CAP, :] = b_t[0:LANES].T.reshape(ne, CAP, LANES)
            tail = b_t[LANES:].T.reshape(ne, groups, rows_g, rest)
            for j in range(groups):
                back[at, CAP:, j * rest : (j + 1) * rest] = tail[:, j]
            to_all(("back", rel), lambda rel, pe: back.at[rel * ne + pe], back_in, back_s.at[rel], back_r.at[rel], rel)
        back_in[e] = back[e]

        gate_out[:, mine] = nt(bin_in[...], gd).astype(BF16)
        up_out[:, mine] = nt(bin_in[...], ud).astype(BF16)
        down_out[:, mine] = nt(bin_t[0], hidden[...].reshape(half, bins)).astype(BF16)
        for s, arrived in enumerate(strips):
            landed(("strip", s))
            n = 2 * len(arrived)
            for i, k in enumerate(arrived):
                c = chunk(k)
                for a in (0, 1):
                    j = 2 * i + a
                    grad_t[a, c] = strip_in[s, j * fc : (j + 1) * fc, :]
                    grad_tr[c, :, a * rest : (a + 1) * rest] = strip_in[
                        s, n * fc : (n + 1) * fc, j * rest : (j + 1) * rest
                    ]
        tails = grad_tr[...].reshape(half, 2 * rest).T
        for a, out in enumerate((gate_out, up_out)):
            out[0:LANES, theirs] = grad_t[a].reshape(half, LANES).T
            out[LANES:, theirs] = tails[a * rest : (a + 1) * rest]

        for rel in (1, 0):
            bulk.pop(("back", rel)).wait()
        for rel in (0, 1):
            for j in range(groups):
                tok_r[:, j * rows_g : (j + 1) * rows_g, rel * rest : (rel + 1) * rest] = back_in[
                    rel * ne : (rel + 1) * ne, CAP:, j * rest : (j + 1) * rest
                ]
        token = 0.0
        for rel in (0, 1):
            token += nn(pick[...], back_in[rel * ne : (rel + 1) * ne, 0:CAP, :].reshape(ne * CAP, LANES))
        tok_out[0:LANES, :] = token.T.astype(BF16)
        tail = nn(pick[...], tok_r[...].reshape(ne * CAP, 2 * rest)).T
        tok_out[LANES:, :] = (tail[0:rest] + tail[rest:]).astype(BF16)
        landed("down_grad")

    work()

    for copy in bulk.values():
        copy.wait()
    for copy in sends:
        copy.wait_send()


def finish(*refs):
    n = len(refs) // 3
    ins, outs, held, sems = refs[0:n], refs[n : 2 * n], refs[2 * n : 3 * n], refs[-1]
    reads = [pltpu.make_async_copy(ins[i], held[i], sems.at[i]) for i in range(n)]
    writes = [pltpu.make_async_copy(held[i], outs[i], sems.at[n + i]) for i in range(n)]
    for copy in reads:
        copy.start()
    for i in range(n):
        reads[i].wait()
        writes[i].start()
    for copy in writes:
        copy.wait()


def layer(ne, nz, *args):
    tg, combine, routes, bin_in, gate_pre, up_pre, gate_w, up_w, down_w = args
    bin_in, gate_pre, up_pre, gate_w, up_w, down_w = (
        a.reshape(a.shape[1:]) for a in (bin_in, gate_pre, up_pre, gate_w, up_w, down_w)
    )
    tg, combine, routes, bin_in = tg.T, combine.T, routes.T, bin_in.T
    width, tokens = tg.shape
    fc, bins = gate_pre.shape
    half, ff = fc * nz, gate_w.shape[1]
    nu, nd = nz // 2, nz - 1 - nz // 2
    rest = width - LANES
    groups = LANES // rest
    block = CAP + CAP // groups
    dma = pltpu.SemaphoreType.DMA

    def v(*shape, dtype=BF16):
        return pltpu.VMEM(shape, dtype)

    scratch = [
        v(*tg.shape), v(*combine.shape, dtype=F32), v(*routes.shape, dtype=jnp.int32),
        v(width, bins), v(width, half), v(width, half), v(width, half),
        v(ne, CAP, tokens, dtype=F32), v(tokens, ne * CAP), v(3, ne, CAP, tokens), v(LANES, groups * tokens),
        v(ne, block, LANES), v(2 * ne, block, LANES), v(ne, CAP, 2 * rest),
        v(2 * ne, block, LANES), v(2 * ne, block, LANES), v(ne, CAP, 2 * rest),
        v(width, half), v(width, half), v(width, half), v(width, bins),
        v(half, 2 * LANES), v(half, 2 * rest), v(bins, 2 * LANES), v(2, width, bins), v(nz, fc, bins, dtype=F32),
        v(nu, fc, bins), v(nd, fc, bins), v(fc, bins), v(fc, bins),
        v(nz, fc, bins), v(nz, fc, bins), v(nz, fc, bins),
        v(nz, fc, bins, dtype=F32), v(nz, fc, bins, dtype=F32), v(nz, fc, bins),
        v(nz, fc, bins), v(nz, fc, bins),
        v(width, half), v(nu + 1, 5 * fc, LANES), v(nu + 1, 5 * fc, LANES),
        v(2, nz, fc, LANES), v(nz, fc, 2 * rest),
        dma((6, nu)), dma((6, nu)), dma((6, nu)), dma((6, nu)),
        dma, dma, dma((2,)), dma((2,)), dma((5,)), dma((5,)), dma((nu + 1,)), dma((nu + 1,)), dma((9,)),
    ]
    grad = jax.ShapeDtypeStruct((width, ff), BF16)
    outs = (jax.ShapeDtypeStruct((width, tokens), BF16), grad, grad, grad)
    vmem, hbm = pl.BlockSpec(memory_space=pltpu.VMEM), pl.BlockSpec(memory_space=pl.ANY)
    made = pl.pallas_call(
        functools.partial(kernel, ne, nz),
        out_shape=outs,
        in_specs=[pl.BlockSpec(memory_space=pltpu.HBM)] * 9,
        out_specs=(vmem,) * 4,
        scratch_shapes=scratch,
        compiler_params=pltpu.CompilerParams(
            collective_id=0, has_side_effects=True, vmem_limit_bytes=58 * 2**20
        ),
        cost_estimate=pl.CostEstimate(
            flops=12 * width * ff * bins, bytes_accessed=6 * 2**20, transcendentals=half * bins
        ),
    )(tg, combine, routes, bin_in, gate_pre, up_pre, gate_w, up_w, down_w)
    made = pl.pallas_call(
        finish,
        out_shape=outs,
        in_specs=[hbm] * 4,
        out_specs=(hbm,) * 4,
        scratch_shapes=[v(width, tokens), v(width, ff), v(width, ff), v(width, ff), dma((8,))],
    )(*made)
    token, gate, up, down = made
    return token.T, gate[None], up[None], down[None]


def solution(mesh):
    ne, nz = mesh.shape["expert"], mesh.shape["tensor"] // 2
    return jax.shard_map(
        functools.partial(layer, ne, nz),
        mesh=mesh,
        in_specs=(
            P("expert", "tensor"),
            P("expert", None),
            P("expert", None),
            P("expert", None, "tensor"),
            P("expert", "tensor", None),
            P("expert", "tensor", None),
            P("expert", "tensor", None),
            P("expert", "tensor", None),
            P("expert", "tensor", None),
        ),
        out_specs=(
            P("expert", "tensor"),
            P("expert", "tensor", None),
            P("expert", "tensor", None),
            P("expert", "tensor", None),
        ),
        check_vma=False,
    )
```
